768 devices in a mesh: dp: 96 (over y_lo, z, core), fsdp: 8 (over y_hi, x).
Axes of the slice: x: 4, y: 8 (y_hi: 2, y_lo: 4; y = y_hi * 4 + y_lo), z: 12, core: 2. Of those that a mesh axis runs over, the one named last changes fastest.
Arguments:
- queries: bfloat16 [49152, 3072], P('dp', 'fsdp'), may hold values from -64 to 64
- key_rows: bfloat16 [49152, 3072], P('dp', 'fsdp'), may hold values from -16 to 16
- value_rows: bfloat16 [49152, 3072], P('dp', 'fsdp'), may hold values from -6 to 6
- segments: int32 [49152], P('dp'), may hold values from 0 to 384, as said below
- send_block: int32 [384], P('dp'), may hold values from 0 to 1, as said below
- out_weight: bfloat16 [3072, 6144], P('fsdp'), may hold values from -0.15625 to 0.15625
- grad_attended: bfloat16 [49152, 3072], P('dp', 'fsdp'), may hold values from -6 to 6
Outputs:
- layer_out: bfloat16 [49152, 6144], P('dp', 'fsdp')
- grad_queries: bfloat16 [49152, 3072], P('dp', 'fsdp')
- grad_keys: bfloat16 [49152, 3072], P('dp', 'fsdp')
- grad_values: bfloat16 [49152, 3072], P('dp', 'fsdp')
The draws below stay inside these ranges and needn't reach their ends.
Inputs may be any that keep to these rules, and one draw needn't show every extreme that they name: `segments`: each image covers one or two whole blocks of 128 rows of one index of dp and begins at its first block's first row; its id is the index of that block among all 384 blocks, and the rows after its patches carry 96 * 4. A one-block image has 64 to 128 patches, a two-block image 128 + 1 to 256. `send_block`: each index of dp marks exactly 2 of its 4 blocks, and its marked blocks hold whole images.
All inputs are finite; a program needn't handle non-finite values.
Results may differ from the reference program's by a relative error of at most 0.015.
Values may be sent and summed in bfloat16 or wider, within the bound.
A program may use at most 64 MiB of HBM per device.

```python
import math
import jax
import jax.numpy as jnp
from jax import lax

D = 6144
HD = 128
HEADS = 24
BLOCK = 128
NB = 4
MOVE = 2
QW = 3072
TOKENS = 49152
N_DP = 96
N_FSDP = 8


START_TABLE = ((0, 0, 2, 2), (0, 0, 2, 2), (0, 1, 2, 3), (0, 1, 2, 3), (0, 1, 2, 3), (0, 0, 2, 3), (0, 1, 1, 3), (0, 1, 2, 2))


MARK_TABLE = ((1, 1, 0, 0), (0, 0, 1, 1), (1, 1, 0, 0), (0, 1, 1, 0), (0, 0, 1, 1), (0, 0, 1, 1), (1, 0, 0, 1), (1, 1, 0, 0))


def layout(key):
    key = jax.random.fold_in(key, 41)
    first, second, third, fourth = jax.random.split(key, 4)
    device_total = TOKENS // (NB * BLOCK)
    half = device_total // 2
    kinds = jax.random.randint(first, (half,), 0, 3)
    heavy = jax.random.randint(second, (device_total,), 0, 2)
    light = 2 + jax.random.randint(third, (device_total,), 0, 3)
    middle = 5 + jax.random.randint(fourth, (device_total,), 0, 3)
    lower = jnp.where(kinds == 0, heavy[:half], jnp.where(kinds == 1, light[:half], middle[:half]))
    upper = jnp.where(kinds == 0, light[half:], jnp.where(kinds == 1, heavy[half:], middle[half:]))
    return jnp.concatenate([lower, upper]).astype(jnp.int32)


def base_pair(key):
    first, second = jax.random.split(key, 2)
    query_vals = jnp.clip(jax.random.normal(first, (TOKENS, QW), jnp.float32), -6.0, 6.0)
    key_vals = jnp.clip(jax.random.normal(second, (TOKENS, QW), jnp.float32), -6.0, 6.0)
    return (query_vals, key_vals)


def draw_queries(key, part):
    query_vals, key_vals = base_pair(key)
    return query_vals.astype(jnp.bfloat16)


def draw_key_rows(key, part):
    query_vals, key_vals = base_pair(key)
    return key_vals.astype(jnp.bfloat16)


def draw_segments(key, part):
    codes = layout(key)
    key = jax.random.fold_in(key, 11)
    device_total = TOKENS // (NB * BLOCK)
    starts = jnp.array(START_TABLE, jnp.int32)[codes]
    block_ids = jnp.arange(NB, dtype=jnp.int32)
    spans = jnp.sum((starts[:, None, :] == block_ids[None, :, None]).astype(jnp.int32), axis=2)
    lowest = jnp.where(spans == 2, BLOCK + 1, BLOCK // 2).astype(jnp.int32)
    highest = jnp.where(spans == 2, 2 * BLOCK + 1, BLOCK + 1).astype(jnp.int32)
    counts = jax.random.randint(key, (device_total, NB), lowest, highest)
    counts = counts.at[0, 0].set(lowest[0, 0])
    own = jnp.take_along_axis(counts, starts, axis=1)
    position = (block_ids[None, :] - starts)[:, :, None] * BLOCK + jnp.arange(BLOCK, dtype=jnp.int32)[None, None, :]
    image_ids = jnp.arange(device_total, dtype=jnp.int32)[:, None] * NB + starts
    result = jnp.where(position < own[:, :, None], image_ids[:, :, None], device_total * NB)
    return result.reshape(TOKENS).astype(jnp.int32)


def draw_send_block(key, part):
    codes = layout(key)
    return jnp.array(MARK_TABLE, jnp.int32)[codes].reshape(-1).astype(jnp.int32)


def raised(entries, key, source, target, shards_of, factor):
    def block_of(axis_at):
        return (jnp.arange(entries.shape[axis_at]) // (entries.shape[axis_at] // shards_of)).reshape((-1,) + (1,) * (entries.ndim - 1 - axis_at))

    one_side = jax.random.permutation(key, shards_of)[block_of(target)]
    second = (block_of(target) + shards_of // 2) % shards_of
    return jnp.where((block_of(source) == one_side) | (block_of(source) == second), factor * entries, entries)


def shard_levels(key, shape, cuts, least, top_value):
    factor_of, own = 1.0, jax.random.fold_in(key, 6)
    for axis_at, parts in cuts:
        heights = jnp.exp(jax.random.uniform(jax.random.fold_in(own, axis_at), (parts,), jnp.float32, least / len(cuts), top_value / len(cuts)))
        factor_of = factor_of * jnp.repeat(heights, shape[axis_at] // parts).reshape([-1 if axis == axis_at else 1 for axis in range(len(shape))])
    return factor_of


def gaussian(stream_key, dims, scale, bound, shards=(), held_as=jnp.bfloat16):
    values = jax.random.normal(stream_key, dims, jnp.float32) * scale
    if len(shards) > 0:
        values = shard_levels(stream_key, dims, shards, -0.22, 0.18) * values
    return jnp.clip(values, min=-bound, max=bound).astype(held_as)


def bell_draw_with(own_key, extent, spread, reach, cuts, heavy, kind=jnp.bfloat16):
    values = spread * jax.random.normal(own_key, extent, jnp.float32)
    if cuts:
        values = values * shard_levels(own_key, extent, cuts, -0.22, 0.18)
    return jnp.clip(raised(values, jax.random.fold_in(own_key, 3), *heavy), -reach, reach).astype(kind)


def setup_inputs(seed: int = 0) -> dict:
    streams_of = jax.random.split(jax.random.key(seed), 8)
    queries = draw_queries(jax.random.fold_in(streams_of[7], 71), 0)
    key_rows = draw_key_rows(jax.random.fold_in(streams_of[7], 71), 0)
    value_rows = gaussian(streams_of[2], (TOKENS, QW), 1.0, 6.0, ((0, 96), (1, 8)))
    segments = draw_segments(jax.random.fold_in(streams_of[7], 71), 0)
    send_block = draw_send_block(jax.random.fold_in(streams_of[7], 71), 0)
    out_weight = bell_draw_with(streams_of[5], (QW, D), QW ** -0.5, 0.15625, ((0, 8),), (0, 1, 8, 2.0))
    grad_attended = gaussian(streams_of[6], (TOKENS, QW), 1.0, 6.0, ((0, 96), (1, 8)))
    return dict(queries=queries, key_rows=key_rows, value_rows=value_rows, segments=segments, send_block=send_block, out_weight=out_weight, grad_attended=grad_attended)


def pick(source, chosen):
    return source[chosen]

def fill(source, chosen, filler):
    return source.at[chosen].set(filler)

def arrange(blocks, marked):
    outbox = jax.vmap(pick)(blocks, marked)
    incoming = jnp.roll(outbox, -(N_DP // 2), axis=0)
    return jax.vmap(fill)(blocks, marked, incoming)

def device_step(inputs):
    bal_query, bal_key, bal_value, bal_segment, grad_in, out_weight = inputs
    inverse_root = 1.0 / math.sqrt(HD)
    row_total = NB * BLOCK
    query_heads = bal_query.reshape(row_total, HEADS, HD).astype(jnp.float32)
    key_heads = bal_key.reshape(row_total, HEADS, HD).astype(jnp.float32)
    value_heads = bal_value.reshape(row_total, HEADS, HD).astype(jnp.float32)
    scores = jnp.einsum('qhd,khd->hqk', query_heads, key_heads) * inverse_root
    allowed = (bal_segment[:, None] == bal_segment[None, :])[None]
    scores = jnp.where(allowed, scores, -jnp.inf)
    row_top = lax.optimization_barrier(jnp.max(scores, axis=-1, keepdims=True))
    shifted = jnp.exp(scores - row_top)
    weights = shifted / lax.optimization_barrier(jnp.sum(shifted, axis=-1, keepdims=True))
    probabilities = lax.optimization_barrier(weights.astype(jnp.bfloat16)).astype(jnp.float32)
    live_heads = (bal_segment < N_DP * NB).astype(jnp.float32)[:, None, None]
    attended = (jnp.einsum('hqk,khd->qhd', probabilities, value_heads) * live_heads).astype(jnp.bfloat16)
    attended = lax.optimization_barrier(attended)
    pieces = attended.reshape(row_total, N_FSDP, QW // N_FSDP).astype(jnp.float32)
    weight_pieces = out_weight.reshape(N_FSDP, QW // N_FSDP, D).astype(jnp.float32)
    partials = jnp.einsum('rsc,scd->srd', pieces, weight_pieces)
    rounded = lax.optimization_barrier(partials.astype(jnp.bfloat16)).astype(jnp.float32)
    layer_rows = lax.optimization_barrier(jnp.sum(rounded, axis=0)).astype(jnp.bfloat16)
    live_rows = (bal_segment < N_DP * NB).astype(jnp.float32)[:, None]
    grad_live = grad_in.astype(jnp.float32) * live_rows
    grad_heads = grad_live.reshape(row_total, HEADS, HD)
    grad_value = jnp.einsum('hqk,qhd->khd', probabilities, grad_heads).astype(jnp.bfloat16)
    grad_probs = jnp.einsum('qhd,khd->hqk', grad_heads, value_heads)
    row_sums = lax.optimization_barrier(jnp.sum(weights * grad_probs, axis=-1, keepdims=True))
    grad_scores = (weights * (grad_probs - row_sums) * inverse_root).astype(jnp.bfloat16)
    grad_scores = lax.optimization_barrier(grad_scores).astype(jnp.float32)
    grad_query = jnp.einsum('hqk,khd->qhd', grad_scores, key_heads).astype(jnp.bfloat16)
    grad_key = jnp.einsum('hqk,qhd->khd', grad_scores, query_heads).astype(jnp.bfloat16)
    return (layer_rows, grad_query.reshape(row_total, QW), grad_key.reshape(row_total, QW), grad_value.reshape(row_total, QW))

def reference(queries, key_rows, value_rows, segments, send_block, out_weight, grad_attended):
    order_keys = jnp.where(send_block.reshape(N_DP, NB) > 0, 0, 1).astype(jnp.int32)
    marked = jnp.argsort(order_keys, axis=1, stable=True)[:, :MOVE].astype(jnp.int32)

    def to_blocks(source):
        return source.reshape((N_DP, NB, BLOCK) + source.shape[1:])

    def to_rows(source):
        return source.reshape((N_DP, NB * BLOCK) + source.shape[3:])
    bal_query = to_rows(arrange(to_blocks(queries), marked))
    bal_key = to_rows(arrange(to_blocks(key_rows), marked))
    bal_value = to_rows(arrange(to_blocks(value_rows), marked))
    bal_segment = to_rows(arrange(to_blocks(segments), marked))
    grad_in = grad_attended.reshape(N_DP, NB * BLOCK, QW)

    def one_device(inputs):
        return device_step(inputs + (out_weight,))
    outputs = lax.map(one_device, (bal_query, bal_key, bal_value, bal_segment, grad_in))

    def restore(source):
        return arrange(source.reshape(N_DP, NB, BLOCK, QW), marked).reshape(TOKENS, QW)
    return (outputs[0].reshape(TOKENS, D), restore(outputs[1]), restore(outputs[2]), restore(outputs[3]))
```

```python
import functools
import math

import jax
import jax.numpy as jnp
from jax import lax
from jax.experimental import pallas as pl
from jax.experimental.pallas import tpu as pltpu
from jax.sharding import PartitionSpec as P

HD = 128
BLOCK = 128
NB = 4
PAIR = 2 * BLOCK
NX = 4
NYL = 4
MESH = pl.DeviceIdType.MESH
BF16 = jnp.bfloat16
F32 = jnp.float32


def marked_and_kept(flags):
    def two(bits):
        first = jnp.where(bits[0] > 0, 0, jnp.where(bits[1] > 0, 1, 2))
        last = jnp.where(bits[3] > 0, 3, jnp.where(bits[2] > 0, 2, 1))
        return first, last

    on = [jnp.where(flag > 0, 1, 0) for flag in flags]
    return two(on), two([1 - bit for bit in on])


def main_kernel(
    nz,
    send_ref,
    seg_ref,
    q_hbm,
    k_hbm,
    v_hbm,
    w_hbm,
    g_hbm,
    out_hbm,
    dq_hbm,
    dk_hbm,
    dv_hbm,
    q_in,
    k_in,
    v_in,
    g_in,
    qp,
    kp,
    vp,
    gp,
    seg_col,
    weights,
    probs,
    dscore,
    moved_out,
    grad_out,
    grad_arrived,
    relay_kept,
    rows_all,
    w_all,
    acc,
    packed_out,
    dq_out,
    dk_out,
    dv_out,
    load_sem,
    store_sem,
    y_send,
    y_recv,
    x_send,
    x_recv,
    f_send,
    f_recv,
    z_send,
    z_recv,
    s_send,
    s_recv,
):
    width = q_hbm.shape[1]
    heads = width // HD
    cols = w_all.shape[2]
    piece = width // (nz * 2)
    half = nz // 2
    inverse_root = 1.0 / math.sqrt(HD)

    g = lax.axis_index("dp")
    f = lax.axis_index("fsdp")
    per_y = nz * 2
    n_dp = NYL * per_y
    pad_id = n_dp * NB
    yl = g // per_y
    z = (g % per_y) // 2
    c = g % 2
    x = f % NX
    yh = f // NX

    def dev(dp, fsdp):
        return {"dp": dp, "fsdp": fsdp}

    partner = (g + n_dp // 2) % n_dp
    p0 = dev(partner, f)
    p1 = dev(partner, (f + NX) % (2 * NX))
    xs = [dev(g, yh * NX + (x + d) % NX) for d in range(NX)]
    right, left = xs[1], xs[3]
    z_right = dev(yl * per_y + ((z + 1) % nz) * 2 + c, f)
    z_left = dev(yl * per_y + ((z + nz - 1) % nz) * 2 + c, f)
    sibling = dev(g + 1 - 2 * c, f)
    mirror_dp = (NYL - 1 - yl) * per_y + z * 2 + c
    mirrors = [dev(mirror_dp, (1 - yh) * NX + (x + d) % NX) for d in range(NX)]
    others = [p0, p1, xs[1], xs[2], xs[3], z_right, z_left, sibling] + mirrors

    barrier = pltpu.get_barrier_semaphore()
    for other in others:
        pl.semaphore_signal(barrier, inc=1, device_id=other, device_id_type=MESH)

    my_cols = pl.ds(pl.multiple_of(f * cols, 128), cols)
    loads = [
        pltpu.make_async_copy(src, dst, load_sem.at[i])
        for i, (src, dst) in enumerate(
            [
                (q_hbm, q_in),
                (k_hbm, k_in),
                (v_hbm, v_in),
                (g_hbm, g_in),
                (w_hbm.at[:, my_cols], w_all.at[0]),
            ]
        )
    ]
    for load in loads:
        load.start()

    on = [send_ref[t].astype(F32) for t in range(NB)]
    off = [1.0 - flag for flag in on]

    def first_and_second(is_set, is_clear):
        return [
            [(0, is_set[0]), (1, is_clear[0] * is_set[1]), (2, is_clear[0] * is_clear[1])],
            [(3, is_set[3]), (2, is_clear[3] * is_set[2]), (1, is_clear[3] * is_clear[2])],
        ]

    order = first_and_second(off, on) + first_and_second(on, off)

    def pick(source, i):
        total = None
        for t, factor in order[i]:
            block = source(t)
            part = block * jnp.full(block.shape, factor, F32).astype(block.dtype)
            total = part if total is None else total + part
        return total

    def pick_block(ref, i):
        return pick(lambda t: ref[pl.ds(t * BLOCK, BLOCK), :], i)

    sends = []

    def remote(src, dst, ssem, rsem, device):
        copy = pltpu.make_async_remote_copy(
            src_ref=src, dst_ref=dst, send_sem=ssem, recv_sem=rsem, device_id=device, device_id_type=MESH
        )
        return copy

    def go(copy):
        copy.start()
        sends.append(copy)

    seg_rows = []
    for i in range(NB):
        row = pick(lambda t: seg_ref[pl.ds(t, 1), :].astype(F32), i)
        seg_rows.append(row)
        seg_col[i] = jnp.transpose(jnp.broadcast_to(row, (BLOCK, BLOCK)))

    def pack(src, dst, first):
        for i in range(first, first + 2):
            dst[pl.ds(i * BLOCK, BLOCK), :] = pick_block(src, i)

    def forward(pair):
        base = pair * PAIR
        for i in range(2):
            col = seg_col[pair * 2 + i]
            live = jnp.where(col < float(pad_id), 1.0, 0.0)
            allowed = jnp.concatenate(
                [col == seg_rows[pair * 2], col == seg_rows[pair * 2 + 1]], axis=1
            )
            for h in range(heads):
                lanes = pl.ds(h * HD, HD)
                q = qp[pl.ds(base + i * BLOCK, BLOCK), lanes]
                k = kp[pl.ds(base, PAIR), lanes]
                v = vp[pl.ds(base, PAIR), lanes]
                scores = (
                    lax.dot_general(q, k, (((1,), (1,)), ((), ())), preferred_element_type=F32)
                    * inverse_root
                )
                scores = jnp.where(allowed, scores, -jnp.inf)
                top = jnp.max(scores, axis=1, keepdims=True)
                raised = jnp.exp(scores - top)
                share = raised * (1.0 / jnp.sum(raised, axis=1, keepdims=True))
                rounded = share.astype(BF16)
                weights[pair * heads + h, pl.ds(i * BLOCK, BLOCK), :] = share
                probs[pair * heads + h, pl.ds(i * BLOCK, BLOCK), :] = rounded
                mixed = jnp.dot(rounded, v, preferred_element_type=F32)
                mixed = (mixed * live).astype(BF16)
                if pair == 1:
                    moved_out[pl.ds(i * BLOCK, BLOCK), lanes] = mixed
                else:
                    rows_all[0, pl.ds(i * BLOCK, BLOCK), lanes] = mixed

    def backward(pair):
        base = pair * PAIR
        for h in range(heads):
            lanes = pl.ds(h * HD, HD)
            tile = pair * heads + h
            q = qp[pl.ds(base, PAIR), lanes]
            k = kp[pl.ds(base, PAIR), lanes]
            v = vp[pl.ds(base, PAIR), lanes]
            for i in range(2):
                rows = pl.ds(i * BLOCK, BLOCK)
                grad = gp[pl.ds(base + i * BLOCK, BLOCK), lanes]
                grad_probs = lax.dot_general(grad, v, (((1,), (1,)), ((), ())), preferred_element_type=F32)
                share = weights[tile, rows, :]
                row_sums = jnp.sum(share * grad_probs, axis=1, keepdims=True)
                grad_scores = (share * (grad_probs - row_sums) * inverse_root).astype(BF16)
                dscore[rows, :] = grad_scores
                dq = jnp.dot(grad_scores, k, preferred_element_type=F32)
                dq_out[pl.ds(base + i * BLOCK, BLOCK), lanes] = dq.astype(BF16)
            grad = gp[pl.ds(base, PAIR), lanes]
            over_rows = (((0,), (0,)), ((), ()))
            dk = lax.dot_general(dscore[...], q, over_rows, preferred_element_type=F32)
            dk_out[pl.ds(base, PAIR), lanes] = dk.astype(BF16)
            dv = lax.dot_general(probs[tile], grad, over_rows, preferred_element_type=F32)
            dv_out[pl.ds(base, PAIR), lanes] = dv.astype(BF16)

    stores = []

    def store_grads(pair):
        rows = pl.ds(pair * PAIR, PAIR)
        for i, (src, dst) in enumerate([(dq_out, dq_hbm), (dk_out, dk_hbm), (dv_out, dv_hbm)]):
            copy = pltpu.make_async_copy(src.at[rows, :], dst.at[rows, :], store_sem.at[pair * 3 + i])
            copy.start()
            stores.append(copy)

    def live_grad(i, block):
        live = jnp.where(seg_col[i] < float(pad_id), 1.0, 0.0).astype(BF16)
        for h in range(heads):
            lanes = pl.ds(h * HD, HD)
            gp[pl.ds(i * BLOCK, BLOCK), lanes] = block[:, h * HD : (h + 1) * HD] * live

    for load in loads[:3]:
        load.wait()
    for src, dst in ((q_in, qp), (k_in, kp), (v_in, vp)):
        pack(src, dst, 2)
    forward(1)

    pl.semaphore_wait(barrier, len(others))

    def piece_rows(at):
        return pl.ds(pl.multiple_of(at * (2 * piece) + c * piece, 16), piece)

    def fetch(slot, device, owner):
        at = pl.ds(pl.multiple_of(owner * cols, 128), cols)
        return remote(
            w_hbm.at[piece_rows(z), at],
            w_all.at[slot, piece_rows(z), :],
            f_send.at[slot],
            f_recv.at[slot],
            device,
        )

    fetches = {}
    for d in (1, 3, 2):
        fetches[NX - d] = fetch(NX - d, xs[d], yh * NX + (x + d) % NX)
    for d in range(NX):
        slot = NX + (NX - d) % NX
        fetches[slot] = fetch(slot, mirrors[d], (1 - yh) * NX + (x + d) % NX)
    for copy in fetches.values():
        go(copy)

    def block_of(ref, slot, b):
        return ref.at[slot, pl.ds(b * BLOCK, BLOCK), :]

    def two_rows(b):
        return pl.ds(b * BLOCK, BLOCK)

    y_copies = [
        remote(moved_out.at[two_rows(0), :], block_of(rows_all, 0, 2), y_send.at[0], y_recv.at[0], p0),
        remote(moved_out.at[two_rows(1), :], block_of(rows_all, 0, 3), y_send.at[1], y_recv.at[1], p0),
        remote(moved_out.at[two_rows(0), :], block_of(rows_all, NX, 2), y_send.at[2], y_recv.at[2], p1),
        remote(moved_out.at[two_rows(1), :], block_of(rows_all, NX, 3), y_send.at[3], y_recv.at[3], p1),
        remote(block_of(rows_all, 0, 0), relay_kept.at[0], y_send.at[4], y_recv.at[4], p0),
        remote(block_of(rows_all, 0, 1), relay_kept.at[1], y_send.at[5], y_recv.at[5], p1),
        remote(relay_kept.at[0], block_of(rows_all, NX, 0), y_send.at[6], y_recv.at[6], p1),
        remote(relay_kept.at[1], block_of(rows_all, NX, 1), y_send.at[7], y_recv.at[7], p0),
        remote(grad_out, grad_arrived, y_send.at[8], y_recv.at[8], p0),
    ]
    for i in (0, 2, 1, 3):
        go(y_copies[i])

    for src, dst in ((q_in, qp), (k_in, kp), (v_in, vp)):
        pack(src, dst, 0)
    forward(0)
    go(y_copies[4])
    go(y_copies[5])

    groups = [(0, 0), (0, 2), (NX, 2), (NX, 0)]
    x_copies = {}
    for n, (slot, first) in enumerate(groups):
        for b in range(2):
            at = first + b
            sem = (n * 2 + b) * 3
            x_copies[n, b, "r"] = remote(
                block_of(rows_all, slot, at),
                block_of(rows_all, slot + 3, at),
                x_send.at[sem],
                x_recv.at[sem],
                right,
            )
            x_copies[n, b, "l"] = remote(
                block_of(rows_all, slot, at),
                block_of(rows_all, slot + 1, at),
                x_send.at[sem + 1],
                x_recv.at[sem + 1],
                left,
            )
            x_copies[n, b, "far"] = remote(
                block_of(rows_all, slot + (3 if b == 0 else 1), at),
                block_of(rows_all, slot + 2, at),
                x_send.at[sem + 2],
                x_recv.at[sem + 2],
                right if b == 0 else left,
            )

    def x_start(n, b):
        go(x_copies[n, b, "r" if b == 0 else "l"])
        go(x_copies[n, b, "l" if b == 0 else "r"])

    def x_relay(n, b):
        x_copies[n, b, "r" if b == 0 else "l"].wait_recv()
        go(x_copies[n, b, "far"])

    def x_finish(n):
        for b in range(2):
            x_copies[n, b, "l" if b == 0 else "r"].wait_recv()
            x_copies[n, b, "far"].wait_recv()

    x_start(0, 0)
    x_start(0, 1)

    loads[3].wait()
    for i in range(2):
        grad_out[pl.ds(i * BLOCK, BLOCK), :] = pick_block(g_in, 2 + i)
    go(y_copies[8])

    subs = [(1, NX), (NX, 2 * NX)]
    last_step = {("r", 0): half - 1, ("r", 1): half - 2, ("l", 0): half - 2, ("l", 1): half - 1}

    def w_piece(sub, at):
        first, end = subs[sub]
        return w_all.at[pl.ds(first, end - first), piece_rows(at), :]

    z_copies = {}
    s_copies = {}
    for sub in range(2):
        s_copies["own", sub, 0] = (sub * nz, z)
        for way in ("r", "l"):
            for s in range(last_step[way, sub] + 1):
                at = (z + nz - s) % nz if way == "r" else (z + s) % nz
                sem = ((0 if way == "r" else 1) * 2 + sub) * half + s
                z_copies[way, sub, s] = remote(
                    w_piece(sub, at),
                    w_piece(sub, at),
                    z_send.at[sem],
                    z_recv.at[sem],
                    z_right if way == "r" else z_left,
                )
                came = (z + nz - s - 1) % nz if way == "r" else (z + s + 1) % nz
                number = 1 + s if way == "r" else half + 1 + s
                if way == "l" and sub == 1:
                    number = half + s
                s_copies[way, sub, s] = (sub * nz + number, came)
    for key, (sem, at) in list(s_copies.items()):
        sub = key[1]
        s_copies[key] = remote(w_piece(sub, at), w_piece(sub, at), s_send.at[sem], s_recv.at[sem], sibling)

    def ring_start(sub):
        first, end = subs[sub]
        for slot in range(first, end):
            fetches[slot].wait_recv()
        for way in ("r", "l"):
            if (way, sub, 0) in z_copies:
                go(z_copies[way, sub, 0])
        go(s_copies["own", sub, 0])

    def ring_step(sub, s):
        for way in ("r", "l"):
            if (way, sub, s) in z_copies:
                z_copies[way, sub, s].wait_recv()
                if (way, sub, s + 1) in z_copies:
                    go(z_copies[way, sub, s + 1])
                go(s_copies[way, sub, s])

    steps = [(sub, s) for s in range(half) for sub in range(2)]

    def ring_steps(count):
        for _ in range(count):
            if steps:
                ring_step(*steps.pop(0))

    def y_arrived(i):
        y_copies[i].wait_recv()

    def project(pair, slots, init):
        rows = pl.ds(pair * PAIR, PAIR)
        for n in range(0, cols, min(cols, 256)):
            lanes = pl.ds(n, min(cols, 256))
            total = None if init else acc[rows, lanes]
            for slot in slots:
                part = jnp.dot(rows_all[slot, rows, :], w_all[slot, :, lanes], preferred_element_type=F32)
                total = part if total is None else total + part
            acc[rows, lanes] = total

    ring_start(0)
    for i in range(2):
        live_grad(i, pick_block(g_in, i))
    backward(0)
    store_grads(0)
    ring_start(1)
    x_relay(0, 0)
    x_relay(0, 1)
    ring_steps(1)
    y_arrived(0)
    x_start(1, 0)
    y_arrived(2)
    x_start(2, 0)
    ring_steps(1)
    y_arrived(1)
    x_start(1, 1)
    y_arrived(3)
    x_start(2, 1)
    y_arrived(4)
    go(y_copies[6])
    y_arrived(5)
    go(y_copies[7])
    loads[4].wait()
    project(0, [0], True)
    project(1, [0], True)
    ring_steps(1)
    x_relay(1, 0)
    x_relay(2, 0)
    ring_steps(1)
    x_relay(1, 1)
    x_relay(2, 1)
    ring_steps(2)
    y_arrived(6)
    x_start(3, 0)
    y_arrived(7)
    x_start(3, 1)
    ring_steps(2)
    x_relay(3, 0)
    x_relay(3, 1)
    ring_steps(1)
    y_arrived(8)
    for i in range(2):
        live_grad(2 + i, grad_arrived[pl.ds(i * BLOCK, BLOCK), :])
    backward(1)
    store_grads(1)
    ring_steps(2 * half)
    for copy in s_copies.values():
        copy.wait_recv()
    x_finish(0)
    project(0, [1, 2, 3], False)
    x_finish(1)
    project(1, [1, 2, 3], False)
    x_finish(2)
    project(1, [4, 5, 6, 7], False)
    packed_out[pl.ds(PAIR, PAIR), :] = acc[pl.ds(PAIR, PAIR), :].astype(BF16)
    late = pltpu.make_async_copy(
        packed_out.at[pl.ds(PAIR, PAIR), :], out_hbm.at[pl.ds(PAIR, PAIR), :], store_sem.at[6]
    )
    late.start()
    x_finish(3)
    project(0, [4, 5, 6, 7], False)
    packed_out[pl.ds(0, PAIR), :] = acc[pl.ds(0, PAIR), :].astype(BF16)
    last = pltpu.make_async_copy(
        packed_out.at[pl.ds(0, PAIR), :], out_hbm.at[pl.ds(0, PAIR), :], store_sem.at[7]
    )
    last.start()
    for copy in sends:
        copy.wait_send()
    for copy in stores + [late, last]:
        copy.wait()


def place_kernel(send_ref, out_p, dq_p, dk_p, dv_p, out, dq, dk, dv, sem):
    (m0, m1), (k0, k1) = marked_and_kept([send_ref[t] for t in range(NB)])
    copies = []
    for i, t in enumerate([k0, k1, m0, m1]):
        to = pl.ds(pl.multiple_of(t * BLOCK, BLOCK), BLOCK)
        for n, (src, dst) in enumerate([(out_p, out), (dq_p, dq), (dk_p, dk), (dv_p, dv)]):
            copies.append(
                pltpu.make_async_copy(src.at[pl.ds(i * BLOCK, BLOCK), :], dst.at[to, :], sem.at[n * NB + i])
            )
    for copy in copies:
        copy.start()
    for copy in copies:
        copy.wait()


def on_device(nz, queries, key_rows, value_rows, segments, send_block, out_weight, grad_attended):
    rows, width = queries.shape
    cols = out_weight.shape[1] // (2 * NX)
    heads = width // HD
    half = nz // 2
    anywhere = pl.BlockSpec(memory_space=pltpu.HBM)
    wide = jax.ShapeDtypeStruct((rows, cols), BF16)
    narrow = jax.ShapeDtypeStruct((rows, width), BF16)
    dma = pltpu.SemaphoreType.DMA
    packed = pl.pallas_call(
        functools.partial(main_kernel, nz),
        out_shape=(wide, narrow, narrow, narrow),
        in_specs=[
            pl.BlockSpec(memory_space=pltpu.SMEM),
            pl.BlockSpec(memory_space=pltpu.VMEM),
        ]
        + [anywhere] * 5,
        out_specs=(anywhere,) * 4,
        scratch_shapes=[pltpu.VMEM((rows, width), BF16)] * 8
        + [
            pltpu.VMEM((NB, BLOCK, BLOCK), F32),
            pltpu.VMEM((2 * heads, PAIR, PAIR), F32),
            pltpu.VMEM((2 * heads, PAIR, PAIR), BF16),
            pltpu.VMEM((PAIR, PAIR), BF16),
            pltpu.VMEM((PAIR, width), BF16),
            pltpu.VMEM((PAIR, width), BF16),
            pltpu.VMEM((PAIR, width), BF16),
            pltpu.VMEM((2, BLOCK, width), BF16),
            pltpu.VMEM((2 * NX, rows, width), BF16),
            pltpu.VMEM((2 * NX, width, cols), BF16),
            pltpu.VMEM((rows, cols), F32),
            pltpu.VMEM((rows, cols), BF16),
        ]
        + [pltpu.VMEM((rows, width), BF16)] * 3
        + [
            dma((5,)),
            dma((8,)),
            dma((9,)),
            dma((9,)),
            dma((24,)),
            dma((24,)),
            dma((8,)),
            dma((8,)),
            dma((4 * half,)),
            dma((4 * half,)),
            dma((2 * nz,)),
            dma((2 * nz,)),
        ],
        compiler_params=pltpu.CompilerParams(
            collective_id=0, has_side_effects=True, vmem_limit_bytes=60 * 1024 * 1024
        ),
        name="attend_gather_project",
    )(
        send_block,
        segments.reshape(NB, BLOCK),
        queries,
        key_rows,
        value_rows,
        out_weight,
        grad_attended,
    )
    return pl.pallas_call(
        place_kernel,
        out_shape=(wide, narrow, narrow, narrow),
        in_specs=[pl.BlockSpec(memory_space=pltpu.SMEM)] + [anywhere] * 4,
        out_specs=(anywhere,) * 4,
        scratch_shapes=[dma((4 * NB,))],
        name="place_blocks",
    )(send_block, *packed)


def solution(mesh):
    nz = mesh.shape["dp"] // (NYL * 2)
    return jax.shard_map(
        functools.partial(on_device, nz),
        mesh=mesh,
        in_specs=(
            P("dp", "fsdp"),
            P("dp", "fsdp"),
            P("dp", "fsdp"),
            P("dp"),
            P("dp"),
            P("fsdp", None),
            P("dp", "fsdp"),
        ),
        out_specs=(P("dp", "fsdp"),) * 4,
        check_vma=False,
    )
```

```python
import functools
import math

import jax
import jax.numpy as jnp
from jax import lax
from jax.experimental import pallas as pl
from jax.experimental.pallas import tpu as pltpu
from jax.sharding import PartitionSpec as P

HD = 128
BLOCK = 128
NB = 4
PAIR = 2 * BLOCK
NX = 4
NYL = 4
MESH = pl.DeviceIdType.MESH
BF16 = jnp.bfloat16
F32 = jnp.float32


def marked_and_kept(flags):
    def two(bits):
        first = jnp.where(bits[0] > 0, 0, jnp.where(bits[1] > 0, 1, 2))
        last = jnp.where(bits[3] > 0, 3, jnp.where(bits[2] > 0, 2, 1))
        return first, last

    on = [jnp.where(flag > 0, 1, 0) for flag in flags]
    return two(on), two([1 - bit for bit in on])


def main_kernel(
    nz,
    send_ref,
    seg_ref,
    q_hbm,
    k_hbm,
    v_hbm,
    w_hbm,
    g_hbm,
    out_hbm,
    dq_hbm,
    dk_hbm,
    dv_hbm,
    q_in,
    k_in,
    v_in,
    g_in,
    qp,
    kp,
    vp,
    gp,
    seg_col,
    weights,
    probs,
    dscore,
    moved_out,
    grad_out,
    grad_arrived,
    relay_kept,
    rows_all,
    w_all,
    acc,
    packed_out,
    dq_out,
    dk_out,
    dv_out,
    load_sem,
    store_sem,
    y_send,
    y_recv,
    x_send,
    x_recv,
    f_send,
    f_recv,
    z_send,
    z_recv,
    s_send,
    s_recv,
):
    width = q_hbm.shape[1]
    heads = width // HD
    cols = w_all.shape[2]
    piece = width // (nz * 2)
    half = nz // 2
    inverse_root = 1.0 / math.sqrt(HD)

    g = lax.axis_index("dp")
    f = lax.axis_index("fsdp")
    per_y = nz * 2
    n_dp = NYL * per_y
    pad_id = n_dp * NB
    yl = g // per_y
    z = (g % per_y) // 2
    c = g % 2
    x = f % NX
    yh = f // NX

    def dev(dp, fsdp):
        return {"dp": dp, "fsdp": fsdp}

    partner = (g + n_dp // 2) % n_dp
    p0 = dev(partner, f)
    p1 = dev(partner, (f + NX) % (2 * NX))
    xs = [dev(g, yh * NX + (x + d) % NX) for d in range(NX)]
    right, left = xs[1], xs[3]
    z_right = dev(yl * per_y + ((z + 1) % nz) * 2 + c, f)
    z_left = dev(yl * per_y + ((z + nz - 1) % nz) * 2 + c, f)
    sibling = dev(g + 1 - 2 * c, f)
    mirror_dp = (NYL - 1 - yl) * per_y + z * 2 + c
    mirrors = [dev(mirror_dp, (1 - yh) * NX + (x + d) % NX) for d in range(NX)]
    others = [p0, p1, xs[1], xs[2], xs[3], z_right, z_left, sibling] + mirrors

    barrier = pltpu.get_barrier_semaphore()
    for other in others:
        pl.semaphore_signal(barrier, inc=1, device_id=other, device_id_type=MESH)

    my_cols = pl.ds(pl.multiple_of(f * cols, 128), cols)
    loads = [
        pltpu.make_async_copy(src, dst, load_sem.at[i])
        for i, (src, dst) in enumerate(
            [
                (q_hbm, q_in),
                (k_hbm, k_in),
                (v_hbm, v_in),
                (g_hbm, g_in),
                (w_hbm.at[:, my_cols], w_all.at[0]),
            ]
        )
    ]
    for load in loads:
        load.start()

    on = [send_ref[t].astype(F32) for t in range(NB)]
    off = [1.0 - flag for flag in on]

    def first_and_second(is_set, is_clear):
        return [
            [(0, is_set[0]), (1, is_clear[0] * is_set[1]), (2, is_clear[0] * is_clear[1])],
            [(3, is_set[3]), (2, is_clear[3] * is_set[2]), (1, is_clear[3] * is_clear[2])],
        ]

    order = first_and_second(off, on) + first_and_second(on, off)

    def pick(source, i):
        total = None
        for t, factor in order[i]:
            block = source(t)
            part = block * jnp.full(block.shape, factor, F32).astype(block.dtype)
            total = part if total is None else total + part
        return total

    def pick_block(ref, i):
        return pick(lambda t: ref[pl.ds(t * BLOCK, BLOCK), :], i)

    sends = []

    def remote(src, dst, ssem, rsem, device):
        copy = pltpu.make_async_remote_copy(
            src_ref=src, dst_ref=dst, send_sem=ssem, recv_sem=rsem, device_id=device, device_id_type=MESH
        )
        return copy

    def go(copy):
        copy.start()
        sends.append(copy)

    seg_rows = []
    for i in range(NB):
        row = pick(lambda t: seg_ref[pl.ds(t, 1), :].astype(F32), i)
        seg_rows.append(row)
        seg_col[i] = jnp.transpose(jnp.broadcast_to(row, (BLOCK, BLOCK)))

    def pack(src, dst, first):
        for i in range(first, first + 2):
            dst[pl.ds(i * BLOCK, BLOCK), :] = pick_block(src, i)

    def forward(pair):
        base = pair * PAIR
        for i in range(2):
            col = seg_col[pair * 2 + i]
            live = jnp.where(col < float(pad_id), 1.0, 0.0)
            allowed = jnp.concatenate(
                [col == seg_rows[pair * 2], col == seg_rows[pair * 2 + 1]], axis=1
            )
            for h in range(heads):
                lanes = pl.ds(h * HD, HD)
                q = qp[pl.ds(base + i * BLOCK, BLOCK), lanes]
                k = kp[pl.ds(base, PAIR), lanes]
                v = vp[pl.ds(base, PAIR), lanes]
                scores = (
                    lax.dot_general(q, k, (((1,), (1,)), ((), ())), preferred_element_type=F32)
                    * inverse_root
                )
                scores = jnp.where(allowed, scores, -jnp.inf)
                top = jnp.max(scores, axis=1, keepdims=True)
                raised = jnp.exp(scores - top)
                share = raised * (1.0 / jnp.sum(raised, axis=1, keepdims=True))
                rounded = share.astype(BF16)
                weights[pair * heads + h, pl.ds(i * BLOCK, BLOCK), :] = share
                probs[pair * heads + h, pl.ds(i * BLOCK, BLOCK), :] = rounded
                mixed = jnp.dot(rounded, v, preferred_element_type=F32)
                mixed = (mixed * live).astype(BF16)
                if pair == 1:
                    moved_out[pl.ds(i * BLOCK, BLOCK), lanes] = mixed
                else:
                    rows_all[0, pl.ds(i * BLOCK, BLOCK), lanes] = mixed

    def backward(pair):
        base = pair * PAIR
        for h in range(heads):
            lanes = pl.ds(h * HD, HD)
            tile = pair * heads + h
            q = qp[pl.ds(base, PAIR), lanes]
            k = kp[pl.ds(base, PAIR), lanes]
            v = vp[pl.ds(base, PAIR), lanes]
            for i in range(2):
                rows = pl.ds(i * BLOCK, BLOCK)
                grad = gp[pl.ds(base + i * BLOCK, BLOCK), lanes]
                grad_probs = lax.dot_general(grad, v, (((1,), (1,)), ((), ())), preferred_element_type=F32)
                share = weights[tile, rows, :]
                row_sums = jnp.sum(share * grad_probs, axis=1, keepdims=True)
                grad_scores = (share * (grad_probs - row_sums) * inverse_root).astype(BF16)
                dscore[rows, :] = grad_scores
                dq = jnp.dot(grad_scores, k, preferred_element_type=F32)
                dq_out[pl.ds(base + i * BLOCK, BLOCK), lanes] = dq.astype(BF16)
            grad = gp[pl.ds(base, PAIR), lanes]
            over_rows = (((0,), (0,)), ((), ()))
            dk = lax.dot_general(dscore[...], q, over_rows, preferred_element_type=F32)
            dk_out[pl.ds(base, PAIR), lanes] = dk.astype(BF16)
            dv = lax.dot_general(probs[tile], grad, over_rows, preferred_element_type=F32)
            dv_out[pl.ds(base, PAIR), lanes] = dv.astype(BF16)

    stores = []

    def store_grads(pair):
        rows = pl.ds(pair * PAIR, PAIR)
        for i, (src, dst) in enumerate([(dq_out, dq_hbm), (dk_out, dk_hbm), (dv_out, dv_hbm)]):
            copy = pltpu.make_async_copy(src.at[rows, :], dst.at[rows, :], store_sem.at[pair * 3 + i])
            copy.start()
            stores.append(copy)

    def live_grad(i, block):
        live = jnp.where(seg_col[i] < float(pad_id), 1.0, 0.0).astype(BF16)
        for h in range(heads):
            lanes = pl.ds(h * HD, HD)
            gp[pl.ds(i * BLOCK, BLOCK), lanes] = block[:, h * HD : (h + 1) * HD] * live

    pl.semaphore_wait(barrier, len(others))

    def piece_rows(at):
        return pl.ds(pl.multiple_of(at * (2 * piece) + c * piece, 16), piece)

    def fetch(slot, device, owner):
        at = pl.ds(pl.multiple_of(owner * cols, 128), cols)
        return remote(
            w_hbm.at[piece_rows(z), at],
            w_all.at[slot, piece_rows(z), :],
            f_send.at[slot],
            f_recv.at[slot],
            device,
        )

    fetches = {}
    for d in (1, 3, 2):
        fetches[NX - d] = fetch(NX - d, xs[d], yh * NX + (x + d) % NX)
    for d in range(NX):
        slot = NX + (NX - d) % NX
        fetches[slot] = fetch(slot, mirrors[d], (1 - yh) * NX + (x + d) % NX)
    for slot in list(range(NX, 2 * NX)) + list(range(1, NX)):
        go(fetches[slot])

    for load in loads[:3]:
        load.wait()
    for src, dst in ((q_in, qp), (k_in, kp), (v_in, vp)):
        pack(src, dst, 2)
    forward(1)

    def block_of(ref, slot, b):
        return ref.at[slot, pl.ds(b * BLOCK, BLOCK), :]

    def two_rows(b):
        return pl.ds(b * BLOCK, BLOCK)

    y_copies = [
        remote(moved_out.at[two_rows(0), :], block_of(rows_all, 0, 2), y_send.at[0], y_recv.at[0], p0),
        remote(moved_out.at[two_rows(1), :], block_of(rows_all, 0, 3), y_send.at[1], y_recv.at[1], p0),
        remote(moved_out.at[two_rows(0), :], block_of(rows_all, NX, 2), y_send.at[2], y_recv.at[2], p1),
        remote(moved_out.at[two_rows(1), :], block_of(rows_all, NX, 3), y_send.at[3], y_recv.at[3], p1),
        remote(block_of(rows_all, 0, 0), relay_kept.at[0], y_send.at[4], y_recv.at[4], p0),
        remote(block_of(rows_all, 0, 1), relay_kept.at[1], y_send.at[5], y_recv.at[5], p1),
        remote(relay_kept.at[0], block_of(rows_all, NX, 0), y_send.at[6], y_recv.at[6], p1),
        remote(relay_kept.at[1], block_of(rows_all, NX, 1), y_send.at[7], y_recv.at[7], p0),
        remote(grad_out.at[two_rows(0), :], grad_arrived.at[two_rows(0), :], y_send.at[8], y_recv.at[8], p0),
        remote(grad_out.at[two_rows(1), :], grad_arrived.at[two_rows(1), :], y_send.at[9], y_recv.at[9], p0),
    ]
    for i in (0, 2, 1, 3):
        go(y_copies[i])
    loads[3].wait()
    for i in range(2):
        grad_out[pl.ds(i * BLOCK, BLOCK), :] = pick_block(g_in, 2 + i)
    go(y_copies[8])

    for src, dst in ((q_in, qp), (k_in, kp), (v_in, vp)):
        pack(src, dst, 0)
    forward(0)
    go(y_copies[4])
    go(y_copies[5])

    groups = [(0, 0), (0, 2), (NX, 2), (NX, 0)]
    x_copies = {}
    for n, (slot, first) in enumerate(groups):
        for b in range(2):
            at = first + b
            sem = (n * 2 + b) * 3
            x_copies[n, b, "r"] = remote(
                block_of(rows_all, slot, at),
                block_of(rows_all, slot + 3, at),
                x_send.at[sem],
                x_recv.at[sem],
                right,
            )
            x_copies[n, b, "l"] = remote(
                block_of(rows_all, slot, at),
                block_of(rows_all, slot + 1, at),
                x_send.at[sem + 1],
                x_recv.at[sem + 1],
                left,
            )
            x_copies[n, b, "far"] = remote(
                block_of(rows_all, slot + (3 if b == 0 else 1), at),
                block_of(rows_all, slot + 2, at),
                x_send.at[sem + 2],
                x_recv.at[sem + 2],
                right if b == 0 else left,
            )

    def x_start(n, b):
        go(x_copies[n, b, "r" if b == 0 else "l"])
        go(x_copies[n, b, "l" if b == 0 else "r"])

    def x_relay(n, b):
        x_copies[n, b, "r" if b == 0 else "l"].wait_recv()
        go(x_copies[n, b, "far"])

    def x_finish(n):
        for b in range(2):
            x_copies[n, b, "l" if b == 0 else "r"].wait_recv()
            x_copies[n, b, "far"].wait_recv()

    x_start(0, 0)
    x_start(0, 1)

    subs = [(1, NX), (NX, 2 * NX)]
    last_step = {("r", 0): half - 1, ("r", 1): half - 2, ("l", 0): half - 2, ("l", 1): half - 1}

    def w_piece(sub, at):
        first, end = subs[sub]
        return w_all.at[pl.ds(first, end - first), piece_rows(at), :]

    z_copies = {}
    s_copies = {}
    for sub in range(2):
        s_copies["own", sub, 0] = (sub * nz, z)
        for way in ("r", "l"):
            for s in range(last_step[way, sub] + 1):
                at = (z + nz - s) % nz if way == "r" else (z + s) % nz
                sem = ((0 if way == "r" else 1) * 2 + sub) * half + s
                z_copies[way, sub, s] = remote(
                    w_piece(sub, at),
                    w_piece(sub, at),
                    z_send.at[sem],
                    z_recv.at[sem],
                    z_right if way == "r" else z_left,
                )
                came = (z + nz - s - 1) % nz if way == "r" else (z + s + 1) % nz
                number = 1 + s if way == "r" else half + 1 + s
                if way == "l" and sub == 1:
                    number = half + s
                s_copies[way, sub, s] = (sub * nz + number, came)
    for key, (sem, at) in list(s_copies.items()):
        sub = key[1]
        s_copies[key] = remote(w_piece(sub, at), w_piece(sub, at), s_send.at[sem], s_recv.at[sem], sibling)

    def ring_start(sub):
        first, end = subs[sub]
        for slot in range(first, end):
            fetches[slot].wait_recv()
        for way in ("r", "l"):
            if (way, sub, 0) in z_copies:
                go(z_copies[way, sub, 0])
        go(s_copies["own", sub, 0])

    def ring_step(sub, s):
        for way in ("r", "l"):
            if (way, sub, s) in z_copies:
                z_copies[way, sub, s].wait_recv()
                if (way, sub, s + 1) in z_copies:
                    go(z_copies[way, sub, s + 1])
                go(s_copies[way, sub, s])

    steps = [(sub, s) for s in range(half) for sub in range(2)]

    def ring_steps(count):
        for _ in range(count):
            if steps:
                ring_step(*steps.pop(0))

    def y_arrived(i):
        y_copies[i].wait_recv()

    def project(pair, slots, init):
        rows = pl.ds(pair * PAIR, PAIR)
        for n in range(0, cols, min(cols, 256)):
            lanes = pl.ds(n, min(cols, 256))
            total = None if init else acc[rows, lanes]
            for slot in slots:
                part = jnp.dot(rows_all[slot, rows, :], w_all[slot, :, lanes], preferred_element_type=F32)
                total = part if total is None else total + part
            acc[rows, lanes] = total

    ring_start(0)
    for i in range(2):
        live_grad(i, pick_block(g_in, i))
    backward(0)
    store_grads(0)
    ring_start(1)
    x_relay(0, 0)
    x_relay(0, 1)
    ring_steps(1)
    y_arrived(0)
    x_start(1, 0)
    y_arrived(2)
    x_start(2, 0)
    ring_steps(2)
    x_relay(1, 0)
    x_relay(2, 0)
    y_arrived(1)
    x_start(1, 1)
    y_arrived(3)
    x_start(2, 1)
    ring_steps(2)
    x_relay(1, 1)
    x_relay(2, 1)
    ring_steps(1)
    y_arrived(4)
    go(y_copies[6])
    y_arrived(5)
    go(y_copies[7])
    go(y_copies[9])
    loads[4].wait()
    project(0, [0], True)
    project(1, [0], True)
    ring_steps(2)
    y_arrived(6)
    x_start(3, 0)
    y_arrived(7)
    x_start(3, 1)
    ring_steps(2)
    x_relay(3, 0)
    x_relay(3, 1)
    ring_steps(1)
    y_arrived(8)
    y_arrived(9)
    for i in range(2):
        live_grad(2 + i, grad_arrived[pl.ds(i * BLOCK, BLOCK), :])
    backward(1)
    store_grads(1)
    ring_steps(2 * half)
    for copy in s_copies.values():
        copy.wait_recv()
    x_finish(0)
    project(0, [1, 2, 3], False)
    x_finish(1)
    project(1, [1, 2, 3], False)
    x_finish(2)
    project(1, [4, 5, 6, 7], False)
    packed_out[pl.ds(PAIR, PAIR), :] = acc[pl.ds(PAIR, PAIR), :].astype(BF16)
    late = pltpu.make_async_copy(
        packed_out.at[pl.ds(PAIR, PAIR), :], out_hbm.at[pl.ds(PAIR, PAIR), :], store_sem.at[6]
    )
    late.start()
    x_finish(3)
    project(0, [4, 5, 6, 7], False)
    packed_out[pl.ds(0, PAIR), :] = acc[pl.ds(0, PAIR), :].astype(BF16)
    last = pltpu.make_async_copy(
        packed_out.at[pl.ds(0, PAIR), :], out_hbm.at[pl.ds(0, PAIR), :], store_sem.at[7]
    )
    last.start()
    for copy in sends:
        copy.wait_send()
    for copy in stores + [late, last]:
        copy.wait()


def place_kernel(send_ref, out_p, dq_p, dk_p, dv_p, out, dq, dk, dv, sem):
    (m0, m1), (k0, k1) = marked_and_kept([send_ref[t] for t in range(NB)])
    copies = []
    for i, t in enumerate([k0, k1, m0, m1]):
        to = pl.ds(pl.multiple_of(t * BLOCK, BLOCK), BLOCK)
        for n, (src, dst) in enumerate([(out_p, out), (dq_p, dq), (dk_p, dk), (dv_p, dv)]):
            copies.append(
                pltpu.make_async_copy(src.at[pl.ds(i * BLOCK, BLOCK), :], dst.at[to, :], sem.at[n * NB + i])
            )
    for copy in copies:
        copy.start()
    for copy in copies:
        copy.wait()


def on_device(nz, queries, key_rows, value_rows, segments, send_block, out_weight, grad_attended):
    rows, width = queries.shape
    cols = out_weight.shape[1] // (2 * NX)
    heads = width // HD
    half = nz // 2
    anywhere = pl.BlockSpec(memory_space=pltpu.HBM)
    wide = jax.ShapeDtypeStruct((rows, cols), BF16)
    narrow = jax.ShapeDtypeStruct((rows, width), BF16)
    dma = pltpu.SemaphoreType.DMA
    packed = pl.pallas_call(
        functools.partial(main_kernel, nz),
        out_shape=(wide, narrow, narrow, narrow),
        in_specs=[
            pl.BlockSpec(memory_space=pltpu.SMEM),
            pl.BlockSpec(memory_space=pltpu.VMEM),
        ]
        + [anywhere] * 5,
        out_specs=(anywhere,) * 4,
        scratch_shapes=[pltpu.VMEM((rows, width), BF16)] * 8
        + [
            pltpu.VMEM((NB, BLOCK, BLOCK), F32),
            pltpu.VMEM((2 * heads, PAIR, PAIR), F32),
            pltpu.VMEM((2 * heads, PAIR, PAIR), BF16),
            pltpu.VMEM((PAIR, PAIR), BF16),
            pltpu.VMEM((PAIR, width), BF16),
            pltpu.VMEM((PAIR, width), BF16),
            pltpu.VMEM((PAIR, width), BF16),
            pltpu.VMEM((2, BLOCK, width), BF16),
            pltpu.VMEM((2 * NX, rows, width), BF16),
            pltpu.VMEM((2 * NX, width, cols), BF16),
            pltpu.VMEM((rows, cols), F32),
            pltpu.VMEM((rows, cols), BF16),
        ]
        + [pltpu.VMEM((rows, width), BF16)] * 3
        + [
            dma((5,)),
            dma((8,)),
            dma((10,)),
            dma((10,)),
            dma((24,)),
            dma((24,)),
            dma((8,)),
            dma((8,)),
            dma((4 * half,)),
            dma((4 * half,)),
            dma((2 * nz,)),
            dma((2 * nz,)),
        ],
        compiler_params=pltpu.CompilerParams(
            collective_id=0, has_side_effects=True, vmem_limit_bytes=60 * 1024 * 1024
        ),
        name="attend_gather_project",
    )(
        send_block,
        segments.reshape(NB, BLOCK),
        queries,
        key_rows,
        value_rows,
        out_weight,
        grad_attended,
    )
    return pl.pallas_call(
        place_kernel,
        out_shape=(wide, narrow, narrow, narrow),
        in_specs=[pl.BlockSpec(memory_space=pltpu.SMEM)] + [pl.BlockSpec(memory_space=pltpu.VMEM)] * 4,
        out_specs=(anywhere,) * 4,
        scratch_shapes=[dma((4 * NB,))],
        name="place_blocks",
    )(send_block, *packed)


def solution(mesh):
    nz = mesh.shape["dp"] // (NYL * 2)
    return jax.shard_map(
        functools.partial(on_device, nz),
        mesh=mesh,
        in_specs=(
            P("dp", "fsdp"),
            P("dp", "fsdp"),
            P("dp", "fsdp"),
            P("dp"),
            P("dp"),
            P("fsdp", None),
            P("dp", "fsdp"),
        ),
        out_specs=(P("dp", "fsdp"),) * 4,
        check_vma=False,
    )
```

```python
import functools
import math

import jax
import jax.numpy as jnp
from jax import lax
from jax.experimental import pallas as pl
from jax.experimental.pallas import tpu as pltpu
from jax.sharding import PartitionSpec as P

HD = 128
BLOCK = 128
NB = 4
PAIR = 2 * BLOCK
NX = 4
NYL = 4
MESH = pl.DeviceIdType.MESH
BF16 = jnp.bfloat16
F32 = jnp.float32


def marked_and_kept(flags):
    def two(bits):
        first = jnp.where(bits[0] > 0, 0, jnp.where(bits[1] > 0, 1, 2))
        last = jnp.where(bits[3] > 0, 3, jnp.where(bits[2] > 0, 2, 1))
        return first, last

    on = [jnp.where(flag > 0, 1, 0) for flag in flags]
    return two(on), two([1 - bit for bit in on])


def main_kernel(
    nz,
    send_ref,
    seg_ref,
    q_hbm,
    k_hbm,
    v_hbm,
    w_hbm,
    g_hbm,
    out_hbm,
    dq_hbm,
    dk_hbm,
    dv_hbm,
    q_in,
    k_in,
    v_in,
    g_in,
    qp,
    kp,
    vp,
    gp,
    seg_col,
    weights,
    probs,
    dscore,
    moved_out,
    grad_out,
    grad_arrived,
    relay_kept,
    rows_all,
    w_all,
    acc,
    packed_out,
    dq_out,
    dk_out,
    dv_out,
    load_sem,
    store_sem,
    y_send,
    y_recv,
    x_send,
    x_recv,
    f_send,
    f_recv,
    z_send,
    z_recv,
    s_send,
    s_recv,
):
    width = q_hbm.shape[1]
    heads = width // HD
    cols = w_all.shape[2]
    piece = width // (nz * 2)
    half = nz // 2
    inverse_root = 1.0 / math.sqrt(HD)

    g = lax.axis_index("dp")
    f = lax.axis_index("fsdp")
    per_y = nz * 2
    n_dp = NYL * per_y
    pad_id = n_dp * NB
    yl = g // per_y
    z = (g % per_y) // 2
    c = g % 2
    x = f % NX
    yh = f // NX

    def dev(dp, fsdp):
        return {"dp": dp, "fsdp": fsdp}

    partner = (g + n_dp // 2) % n_dp
    p0 = dev(partner, f)
    p1 = dev(partner, (f + NX) % (2 * NX))
    xs = [dev(g, yh * NX + (x + d) % NX) for d in range(NX)]
    right, left = xs[1], xs[3]
    z_right = dev(yl * per_y + ((z + 1) % nz) * 2 + c, f)
    z_left = dev(yl * per_y + ((z + nz - 1) % nz) * 2 + c, f)
    sibling = dev(g + 1 - 2 * c, f)
    mirror_dp = (NYL - 1 - yl) * per_y + z * 2 + c
    mirrors = [dev(mirror_dp, (1 - yh) * NX + (x + d) % NX) for d in range(NX)]
    others = [p0, p1, xs[1], xs[2], xs[3], z_right, z_left, sibling] + mirrors

    barrier = pltpu.get_barrier_semaphore()
    for other in others:
        pl.semaphore_signal(barrier, inc=1, device_id=other, device_id_type=MESH)

    my_cols = pl.ds(pl.multiple_of(f * cols, 128), cols)
    loads = [
        pltpu.make_async_copy(src, dst, load_sem.at[i])
        for i, (src, dst) in enumerate(
            [
                (q_hbm, q_in),
                (k_hbm, k_in),
                (v_hbm, v_in),
                (g_hbm, g_in),
                (w_hbm.at[:, my_cols], w_all.at[0]),
            ]
        )
    ]
    for load in loads:
        load.start()

    on = [send_ref[t].astype(F32) for t in range(NB)]
    off = [1.0 - flag for flag in on]

    def first_and_second(is_set, is_clear):
        return [
            [(0, is_set[0]), (1, is_clear[0] * is_set[1]), (2, is_clear[0] * is_clear[1])],
            [(3, is_set[3]), (2, is_clear[3] * is_set[2]), (1, is_clear[3] * is_clear[2])],
        ]

    order = first_and_second(off, on) + first_and_second(on, off)

    def pick(source, i):
        total = None
        for t, factor in order[i]:
            block = source(t)
            part = block * jnp.full(block.shape, factor, F32).astype(block.dtype)
            total = part if total is None else total + part
        return total

    def pick_block(ref, i):
        return pick(lambda t: ref[pl.ds(t * BLOCK, BLOCK), :], i)

    sends = []

    def remote(src, dst, ssem, rsem, device):
        copy = pltpu.make_async_remote_copy(
            src_ref=src, dst_ref=dst, send_sem=ssem, recv_sem=rsem, device_id=device, device_id_type=MESH
        )
        return copy

    def go(copy):
        copy.start()
        sends.append(copy)

    seg_rows = []
    for i in range(NB):
        row = pick(lambda t: seg_ref[pl.ds(t, 1), :].astype(F32), i)
        seg_rows.append(row)
        seg_col[i] = jnp.transpose(jnp.broadcast_to(row, (BLOCK, BLOCK)))

    def pack(src, dst, first):
        for i in range(first, first + 2):
            dst[pl.ds(i * BLOCK, BLOCK), :] = pick_block(src, i)

    def forward(pair):
        base = pair * PAIR
        for i in range(2):
            col = seg_col[pair * 2 + i]
            live = jnp.where(col < float(pad_id), 1.0, 0.0)
            allowed = jnp.concatenate(
                [col == seg_rows[pair * 2], col == seg_rows[pair * 2 + 1]], axis=1
            )
            for h in range(heads):
                lanes = pl.ds(h * HD, HD)
                q = qp[pl.ds(base + i * BLOCK, BLOCK), lanes]
                k = kp[pl.ds(base, PAIR), lanes]
                v = vp[pl.ds(base, PAIR), lanes]
                scores = (
                    lax.dot_general(q, k, (((1,), (1,)), ((), ())), preferred_element_type=F32)
                    * inverse_root
                )
                scores = jnp.where(allowed, scores, -jnp.inf)
                top = jnp.max(scores, axis=1, keepdims=True)
                raised = jnp.exp(scores - top)
                share = raised * (1.0 / jnp.sum(raised, axis=1, keepdims=True))
                rounded = share.astype(BF16)
                weights[pair * heads + h, pl.ds(i * BLOCK, BLOCK), :] = share
                probs[pair * heads + h, pl.ds(i * BLOCK, BLOCK), :] = rounded
                mixed = jnp.dot(rounded, v, preferred_element_type=F32)
                mixed = (mixed * live).astype(BF16)
                if pair == 1:
                    moved_out[pl.ds(i * BLOCK, BLOCK), lanes] = mixed
                else:
                    rows_all[0, pl.ds(i * BLOCK, BLOCK), lanes] = mixed

    def backward(pair, some):
        base = pair * PAIR
        for h in some:
            lanes = pl.ds(h * HD, HD)
            tile = pair * heads + h
            q = qp[pl.ds(base, PAIR), lanes]
            k = kp[pl.ds(base, PAIR), lanes]
            v = vp[pl.ds(base, PAIR), lanes]
            for i in range(2):
                rows = pl.ds(i * BLOCK, BLOCK)
                grad = gp[pl.ds(base + i * BLOCK, BLOCK), lanes]
                grad_probs = lax.dot_general(grad, v, (((1,), (1,)), ((), ())), preferred_element_type=F32)
                share = weights[tile, rows, :]
                row_sums = jnp.sum(share * grad_probs, axis=1, keepdims=True)
                grad_scores = (share * (grad_probs - row_sums) * inverse_root).astype(BF16)
                dscore[rows, :] = grad_scores
                dq = jnp.dot(grad_scores, k, preferred_element_type=F32)
                dq_out[pl.ds(base + i * BLOCK, BLOCK), lanes] = dq.astype(BF16)
            grad = gp[pl.ds(base, PAIR), lanes]
            over_rows = (((0,), (0,)), ((), ()))
            dk = lax.dot_general(dscore[...], q, over_rows, preferred_element_type=F32)
            dk_out[pl.ds(base, PAIR), lanes] = dk.astype(BF16)
            dv = lax.dot_general(probs[tile], grad, over_rows, preferred_element_type=F32)
            dv_out[pl.ds(base, PAIR), lanes] = dv.astype(BF16)

    stores = []

    def store_grads(pair):
        rows = pl.ds(pair * PAIR, PAIR)
        for i, (src, dst) in enumerate([(dq_out, dq_hbm), (dk_out, dk_hbm), (dv_out, dv_hbm)]):
            copy = pltpu.make_async_copy(src.at[rows, :], dst.at[rows, :], store_sem.at[pair * 3 + i])
            copy.start()
            stores.append(copy)

    def live_grad(i, block):
        live = jnp.where(seg_col[i] < float(pad_id), 1.0, 0.0).astype(BF16)
        for h in range(heads):
            lanes = pl.ds(h * HD, HD)
            gp[pl.ds(i * BLOCK, BLOCK), lanes] = block[:, h * HD : (h + 1) * HD] * live

    pl.semaphore_wait(barrier, len(others))

    def piece_rows(at):
        return pl.ds(pl.multiple_of(at * (2 * piece) + c * piece, 16), piece)

    fetches = {}
    for way, piece_at in (("near", z), ("far", (z + half) % nz)):
        for d in range(2 * NX):
            if d == 0:
                continue
            slot = NX - d if d < NX else NX + (2 * NX - d) % NX
            owner = (yh if d < NX else 1 - yh) * NX + (x + d) % NX
            sem = slot + (2 * NX if way == "far" else 0)
            fetches[way, slot] = remote(
                w_hbm.at[piece_rows(piece_at), pl.ds(pl.multiple_of(owner * cols, 128), cols)],
                w_all.at[slot, piece_rows(piece_at), :],
                f_send.at[sem],
                f_recv.at[sem],
                xs[d] if d < NX else mirrors[d - NX],
            )
    fetch_order = list(range(NX, 2 * NX)) + list(range(1, NX))
    for slot in fetch_order:
        go(fetches["near", slot])

    for load in loads[:3]:
        load.wait()
    for src, dst in ((q_in, qp), (k_in, kp), (v_in, vp)):
        pack(src, dst, 2)
    forward(1)

    def block_of(ref, slot, b):
        return ref.at[slot, pl.ds(b * BLOCK, BLOCK), :]

    def two_rows(b):
        return pl.ds(b * BLOCK, BLOCK)

    y_copies = [
        remote(moved_out.at[two_rows(0), :], block_of(rows_all, 0, 2), y_send.at[0], y_recv.at[0], p0),
        remote(moved_out.at[two_rows(1), :], block_of(rows_all, 0, 3), y_send.at[1], y_recv.at[1], p0),
        remote(moved_out.at[two_rows(0), :], block_of(rows_all, NX, 2), y_send.at[2], y_recv.at[2], p1),
        remote(moved_out.at[two_rows(1), :], block_of(rows_all, NX, 3), y_send.at[3], y_recv.at[3], p1),
        remote(block_of(rows_all, 0, 0), relay_kept.at[0], y_send.at[4], y_recv.at[4], p0),
        remote(block_of(rows_all, 0, 1), relay_kept.at[1], y_send.at[5], y_recv.at[5], p1),
        remote(relay_kept.at[0], block_of(rows_all, NX, 0), y_send.at[6], y_recv.at[6], p1),
        remote(relay_kept.at[1], block_of(rows_all, NX, 1), y_send.at[7], y_recv.at[7], p0),
        remote(grad_out.at[two_rows(0), :], grad_arrived.at[two_rows(0), :], y_send.at[8], y_recv.at[8], p0),
        remote(grad_out.at[two_rows(1), :], grad_arrived.at[two_rows(1), :], y_send.at[9], y_recv.at[9], p0),
    ]
    for i in (0, 2, 1, 3):
        go(y_copies[i])

    for src, dst in ((q_in, qp), (k_in, kp), (v_in, vp)):
        pack(src, dst, 0)
    forward(0)
    go(y_copies[4])
    go(y_copies[5])

    groups = [(0, 0), (0, 2), (NX, 2), (NX, 0)]
    x_copies = {}
    for n, (slot, first) in enumerate(groups):
        for b in range(2):
            at = first + b
            sem = (n * 2 + b) * 3
            x_copies[n, b, "r"] = remote(
                block_of(rows_all, slot, at),
                block_of(rows_all, slot + 3, at),
                x_send.at[sem],
                x_recv.at[sem],
                right,
            )
            x_copies[n, b, "l"] = remote(
                block_of(rows_all, slot, at),
                block_of(rows_all, slot + 1, at),
                x_send.at[sem + 1],
                x_recv.at[sem + 1],
                left,
            )
            x_copies[n, b, "far"] = remote(
                block_of(rows_all, slot + (3 if b == 0 else 1), at),
                block_of(rows_all, slot + 2, at),
                x_send.at[sem + 2],
                x_recv.at[sem + 2],
                right if b == 0 else left,
            )

    def x_start(n, b):
        go(x_copies[n, b, "r" if b == 0 else "l"])
        go(x_copies[n, b, "l" if b == 0 else "r"])

    def x_relay(n, b):
        x_copies[n, b, "r" if b == 0 else "l"].wait_recv()
        go(x_copies[n, b, "far"])

    def x_finish(n):
        for b in range(2):
            x_copies[n, b, "l" if b == 0 else "r"].wait_recv()
            x_copies[n, b, "far"].wait_recv()

    x_start(0, 0)
    x_start(0, 1)
    loads[3].wait()
    for i in range(2):
        grad_out[pl.ds(i * BLOCK, BLOCK), :] = pick_block(g_in, 2 + i)
    go(y_copies[8])
    go(y_copies[9])

    subs = [(1, NX), (NX, 2 * NX)]

    def w_piece(sub, at):
        first, end = subs[sub]
        return w_all.at[pl.ds(first, end - first), piece_rows(at), :]

    def to_sibling(sub, number, at):
        sem = sub * nz + number
        return remote(w_piece(sub, at), w_piece(sub, at), s_send.at[sem], s_recv.at[sem], sibling)

    z_copies = {}
    s_copies = {}
    for sub in range(2):
        s_copies["near", sub, 0] = to_sibling(sub, 0, z)
        s_copies["far", sub, 0] = to_sibling(sub, 1, (z + half) % nz)
        for n, way in enumerate(("r", "l")):
            for s in range(half - 1):
                at = (z + nz - s) % nz if way == "r" else (z + s) % nz
                came = (z + nz - s - 1) % nz if way == "r" else (z + s + 1) % nz
                sem = (n * 2 + sub) * half + s
                z_copies[way, sub, s] = remote(
                    w_piece(sub, at),
                    w_piece(sub, at),
                    z_send.at[sem],
                    z_recv.at[sem],
                    z_right if way == "r" else z_left,
                )
                s_copies[way, sub, s] = to_sibling(sub, 2 + n * (half - 1) + s, came)

    def fetched(way, sub):
        first, end = subs[sub]
        for slot in range(first, end):
            fetches[way, slot].wait_recv()

    def ring_start(sub):
        fetched("near", sub)
        for way in ("r", "l"):
            if (way, sub, 0) in z_copies:
                go(z_copies[way, sub, 0])
        go(s_copies["near", sub, 0])

    def ring_step(sub, s):
        if s >= half - 1:
            return
        for way in ("r", "l"):
            z_copies[way, sub, s].wait_recv()
            if (way, sub, s + 1) in z_copies:
                go(z_copies[way, sub, s + 1])
        for way in ("r", "l"):
            go(s_copies[way, sub, s])

    def far_arrived(sub):
        fetched("far", sub)
        go(s_copies["far", sub, 0])

    def sub_complete(sub):
        for key, copy in s_copies.items():
            if key[1] == sub:
                copy.wait_recv()

    def y_arrived(i):
        y_copies[i].wait_recv()

    def project(pair, slots, init):
        rows = pl.ds(pair * PAIR, PAIR)
        for n in range(0, cols, min(cols, 256)):
            lanes = pl.ds(n, min(cols, 256))
            total = None if init else acc[rows, lanes]
            for slot in slots:
                part = jnp.dot(rows_all[slot, rows, :], w_all[slot, :, lanes], preferred_element_type=F32)
                total = part if total is None else total + part
            acc[rows, lanes] = total

    ring_start(0)
    for slot in fetch_order:
        go(fetches["far", slot])
    for i in range(2):
        live_grad(i, pick_block(g_in, i))
    backward(0, range(0, heads - 1))
    x_relay(0, 0)
    x_relay(0, 1)
    backward(0, range(heads - 1, heads))
    store_grads(0)
    ring_start(1)
    ring_step(0, 0)
    y_arrived(0)
    x_start(1, 0)
    y_arrived(2)
    x_start(2, 0)
    ring_step(1, 0)
    ring_step(0, 1)
    x_relay(1, 0)
    x_relay(2, 0)
    y_arrived(1)
    x_start(1, 1)
    y_arrived(3)
    x_start(2, 1)
    ring_step(1, 1)
    y_arrived(4)
    go(y_copies[6])
    y_arrived(5)
    go(y_copies[7])
    ring_step(0, 2)
    x_relay(1, 1)
    x_relay(2, 1)
    far_arrived(0)
    far_arrived(1)
    y_arrived(8)
    y_arrived(9)
    for i in range(2):
        live_grad(2 + i, grad_arrived[pl.ds(i * BLOCK, BLOCK), :])
    ring_step(1, 2)
    backward(1, range(0, 1))
    ring_step(0, 3)
    y_arrived(6)
    x_start(3, 0)
    y_arrived(7)
    x_start(3, 1)
    backward(1, range(1, min(2, heads)))
    ring_step(1, 3)
    x_relay(3, 0)
    x_relay(3, 1)
    backward(1, range(2, heads))
    store_grads(1)
    loads[4].wait()
    project(0, [0], True)
    project(1, [0], True)
    ring_step(0, 4)
    for s in range(5, half):
        ring_step(0, s)
    x_finish(0)
    x_finish(1)
    sub_complete(0)
    project(0, [1, 2, 3], False)
    project(1, [1, 2, 3], False)
    for s in range(4, half):
        ring_step(1, s)
    x_finish(2)
    sub_complete(1)
    project(1, [4, 5, 6, 7], False)
    packed_out[pl.ds(PAIR, PAIR), :] = acc[pl.ds(PAIR, PAIR), :].astype(BF16)
    late = pltpu.make_async_copy(
        packed_out.at[pl.ds(PAIR, PAIR), :], out_hbm.at[pl.ds(PAIR, PAIR), :], store_sem.at[6]
    )
    late.start()
    x_finish(3)
    project(0, [4, 5, 6, 7], False)
    packed_out[pl.ds(0, PAIR), :] = acc[pl.ds(0, PAIR), :].astype(BF16)
    last = pltpu.make_async_copy(
        packed_out.at[pl.ds(0, PAIR), :], out_hbm.at[pl.ds(0, PAIR), :], store_sem.at[7]
    )
    last.start()
    for copy in sends:
        copy.wait_send()
    for copy in stores + [late, last]:
        copy.wait()


def place_kernel(send_ref, out_p, dq_p, dk_p, dv_p, out, dq, dk, dv, sem):
    (m0, m1), (k0, k1) = marked_and_kept([send_ref[t] for t in range(NB)])
    copies = []
    for i, t in enumerate([k0, k1, m0, m1]):
        to = pl.ds(pl.multiple_of(t * BLOCK, BLOCK), BLOCK)
        for n, (src, dst) in enumerate([(out_p, out), (dq_p, dq), (dk_p, dk), (dv_p, dv)]):
            copies.append(
                pltpu.make_async_copy(src.at[pl.ds(i * BLOCK, BLOCK), :], dst.at[to, :], sem.at[n * NB + i])
            )
    for copy in copies:
        copy.start()
    for copy in copies:
        copy.wait()


def on_device(nz, queries, key_rows, value_rows, segments, send_block, out_weight, grad_attended):
    rows, width = queries.shape
    cols = out_weight.shape[1] // (2 * NX)
    heads = width // HD
    half = nz // 2
    anywhere = pl.BlockSpec(memory_space=pltpu.HBM)
    wide = jax.ShapeDtypeStruct((rows, cols), BF16)
    narrow = jax.ShapeDtypeStruct((rows, width), BF16)
    dma = pltpu.SemaphoreType.DMA
    packed = pl.pallas_call(
        functools.partial(main_kernel, nz),
        out_shape=(wide, narrow, narrow, narrow),
        in_specs=[
            pl.BlockSpec(memory_space=pltpu.SMEM),
            pl.BlockSpec(memory_space=pltpu.VMEM),
        ]
        + [anywhere] * 5,
        out_specs=(anywhere,) * 4,
        scratch_shapes=[pltpu.VMEM((rows, width), BF16)] * 8
        + [
            pltpu.VMEM((NB, BLOCK, BLOCK), F32),
            pltpu.VMEM((2 * heads, PAIR, PAIR), F32),
            pltpu.VMEM((2 * heads, PAIR, PAIR), BF16),
            pltpu.VMEM((PAIR, PAIR), BF16),
            pltpu.VMEM((PAIR, width), BF16),
            pltpu.VMEM((PAIR, width), BF16),
            pltpu.VMEM((PAIR, width), BF16),
            pltpu.VMEM((2, BLOCK, width), BF16),
            pltpu.VMEM((2 * NX, rows, width), BF16),
            pltpu.VMEM((2 * NX, width, cols), BF16),
            pltpu.VMEM((rows, cols), F32),
            pltpu.VMEM((rows, cols), BF16),
        ]
        + [pltpu.VMEM((rows, width), BF16)] * 3
        + [
            dma((5,)),
            dma((8,)),
            dma((10,)),
            dma((10,)),
            dma((24,)),
            dma((24,)),
            dma((4 * NX,)),
            dma((4 * NX,)),
            dma((4 * half,)),
            dma((4 * half,)),
            dma((2 * nz,)),
            dma((2 * nz,)),
        ],
        compiler_params=pltpu.CompilerParams(
            collective_id=0, has_side_effects=True, vmem_limit_bytes=60 * 1024 * 1024
        ),
        name="attend_gather_project",
    )(
        send_block,
        segments.reshape(NB, BLOCK),
        queries,
        key_rows,
        value_rows,
        out_weight,
        grad_attended,
    )
    return pl.pallas_call(
        place_kernel,
        out_shape=(wide, narrow, narrow, narrow),
        in_specs=[pl.BlockSpec(memory_space=pltpu.SMEM)] + [pl.BlockSpec(memory_space=pltpu.VMEM)] * 4,
        out_specs=(anywhere,) * 4,
        scratch_shapes=[dma((4 * NB,))],
        name="place_blocks",
    )(send_block, *packed)


def solution(mesh):
    nz = mesh.shape["dp"] // (NYL * 2)
    return jax.shard_map(
        functools.partial(on_device, nz),
        mesh=mesh,
        in_specs=(
            P("dp", "fsdp"),
            P("dp", "fsdp"),
            P("dp", "fsdp"),
            P("dp"),
            P("dp"),
            P("fsdp", None),
            P("dp", "fsdp"),
        ),
        out_specs=(P("dp", "fsdp"),) * 4,
        check_vma=False,
    )
```
